512 devices in a mesh: replica: 32 (over y, z_hi), tensor: 16 (over x, z_lo, core).
Axes of the slice: x: 4, y: 8, z: 8 (z_hi: 4, z_lo: 2; z = z_hi * 2 + z_lo), core: 2. Of those that a mesh axis runs over, the one named last changes fastest.
Arguments:
- activations: bfloat16 [32, 3072, 4096], P('replica', 'tensor'), may hold values from -6 to 6
- cotangent: bfloat16 [32, 3072, 512], P('replica', 'tensor'), may hold values from -6 to 6
- weight: float32 [32, 4096, 512], P('replica', 'tensor'), may hold values from -6 to 6
- first_moment: float32 [32, 4096, 512], P('replica', 'tensor'), may hold values from -3 to 3
- second_moment: float32 [32, 4096, 512], P('replica', 'tensor'), may hold values from 0.05 to 2
- anchor: float32 [4096, 512], P('tensor', 'replica'), may hold values from -6 to 6
- outer_momentum: float32 [4096, 512], P('tensor', 'replica'), may hold values from -2 to 2
- fragment_rows: int32 [4096], P('tensor'), may hold values 0 or 1
Outputs:
- weight_out: float32 [32, 4096, 512], P('replica', 'tensor')
- first_out: float32 [32, 4096, 512], P('replica', 'tensor')
- second_out: float32 [32, 4096, 512], P('replica', 'tensor')
- anchor_out: float32 [4096, 512], P('tensor', 'replica')
- momentum_out: float32 [4096, 512], P('tensor', 'replica')
- projected: bfloat16 [32, 3072, 512], P('replica', 'tensor')
The draws below stay inside these ranges and needn't reach their ends.
All inputs are finite; a program needn't handle non-finite values. No bound on the sum of `fragment_rows` on one device may be relied on, other than what follows from the above.
Results may differ from the reference program's by a relative error of at most 0.011.
Values may be sent and summed in bfloat16 or wider, within the bound.
A program may use at most 64 MiB of HBM per device.

```python
import math
import jax
import jax.numpy as jnp
from jax import lax

D = 4096
C = 512
STEP = 20
TOKENS = 3072
REPLICAS = 32
N_REPLICA = 32
N_TENSOR = 16


def place_ends(drawn, own_key, least, largest):
    spot = [jax.random.randint(jax.random.fold_in(own_key, axis), (), 0, length) for axis, length in enumerate(drawn.shape)]
    longest = drawn.shape.index(max(drawn.shape))
    neighbour = spot[:longest] + [(spot[longest] + 1) % drawn.shape[longest]] + spot[longest + 1:]
    return drawn.at[tuple(spot)].set(least).at[tuple(neighbour)].set(largest)


def with_spikes(array, key, source, target, blocks, factor):
    owner, partner = [(jnp.arange(array.shape[position]) // (array.shape[position] // blocks)).reshape([-1 if axis == position else 1 for axis in range(array.ndim)]) for position in (source, target)]
    chosen = jax.random.permutation(key, blocks)[partner]
    strong = (owner == chosen) | (owner == (partner + blocks // 2) % blocks)
    return jnp.where(strong, factor * array, array)


def levels(rng, extent, shards, smallest, largest):
    def one(dim, blocks):
        draws = jax.random.uniform(jax.random.fold_in(jax.random.fold_in(rng, 6), dim), (blocks,), jnp.float32, smallest / len(shards), largest / len(shards))
        return jnp.repeat(jnp.exp(draws), extent[dim] // blocks).reshape((-1,) + (1,) * (len(extent) - dim - 1))

    factor_of = one(*shards[0])
    for cut in shards[1:]:
        factor_of = factor_of * one(*cut)
    return factor_of


def scatter_about(rng, extent, deviation, bound, split=(), dtype=jnp.bfloat16):
    array = jax.random.normal(rng, extent, jnp.float32) * deviation
    if len(split) > 0:
        array = levels(rng, extent, split, -0.22, 0.18) * array
    return jnp.clip(array, min=-bound, max=bound).astype(dtype)


def gaussian_with(own_key, shape, spread, reach, pieces, heavy, kind=jnp.bfloat16):
    array = spread * jax.random.normal(own_key, shape, jnp.float32)
    if pieces:
        array = array * levels(own_key, shape, pieces, -0.22, 0.18)
    return jnp.clip(with_spikes(array, jax.random.fold_in(own_key, 3), *heavy), -reach, reach).astype(kind)


def setup_inputs(seed: int = 0) -> dict:
    arg_keys = jax.random.split(jax.random.key(seed), 9)
    activations = scatter_about(arg_keys[0], (REPLICAS, TOKENS, D), 1.0, 6.0, ((0, 32), (1, 16)))
    cotangent = scatter_about(arg_keys[1], (REPLICAS, TOKENS, C), 1.0, 6.0, ((0, 32), (1, 16)))
    weight = gaussian_with(arg_keys[2], (REPLICAS, D, C), 1.0, 6.0, ((0, 32), (1, 16)), (0, 2, 32, 2.75), jnp.float32)
    first_moment = scatter_about(arg_keys[3], (REPLICAS, D, C), 0.5, 3.0, ((0, 32), (1, 16)), jnp.float32)
    second_moment = jnp.clip(jnp.exp(math.log(2.0) - 3.6888794 * jax.random.uniform(arg_keys[4], (REPLICAS, D, C), jnp.float32) ** levels(arg_keys[4], (REPLICAS, D, C), ((0, 32), (1, 16)), -0.2, 0.2)), 0.05, 2.0)
    anchor = scatter_about(arg_keys[5], (D, C), 1.0, 6.0, ((0, 16), (1, 32)), jnp.float32)
    outer_momentum = scatter_about(arg_keys[6], (D, C), 0.3, 2.0, ((0, 16), (1, 32)), jnp.float32)
    fragment_rows = place_ends((jax.random.randint(arg_keys[7], (D,), 0, 2) < 1).astype(jnp.int32), jax.random.fold_in(arg_keys[7], 1), 0, 1)
    return {"activations": activations, "cotangent": cotangent, "weight": weight, "first_moment": first_moment, "second_moment": second_moment, "anchor": anchor, "outer_momentum": outer_momentum, "fragment_rows": fragment_rows}


FIRST_DECAY = 0.9
SECOND_DECAY = 0.95
ADAM_EPS = 1e-08
INNER_RATE = 0.02
WEIGHT_DECAY = 0.1
OUTER_RATE = 0.7
OUTER_MU = 0.9
MIX_SHARE = 0.5

def replica_step(operands):
    inputs_here, cotan_here, weight_here, first_here, second_here = operands
    multiplier = D ** (-0.5)
    block_width = D // N_TENSOR
    weight_low = weight_here.astype(jnp.bfloat16)
    split_inputs = inputs_here.reshape(TOKENS, N_TENSOR, block_width).astype(jnp.float32)
    split_weight = weight_low.reshape(N_TENSOR, block_width, C).astype(jnp.float32)
    partial_value = jnp.einsum('tkd,kdc->ktc', split_inputs, split_weight) * multiplier
    projected = lax.optimization_barrier(jnp.sum(partial_value, axis=0)).astype(jnp.bfloat16)
    gradient = jnp.dot(inputs_here.T, cotan_here, preferred_element_type=jnp.float32) * multiplier
    first_new = FIRST_DECAY * first_here + (1.0 - FIRST_DECAY) * gradient
    second_new = SECOND_DECAY * second_here + (1.0 - SECOND_DECAY) * gradient * gradient
    first_hat = first_new / (1.0 - FIRST_DECAY ** STEP)
    second_hat = second_new / (1.0 - SECOND_DECAY ** STEP)
    update = first_hat / (jnp.sqrt(second_hat) + ADAM_EPS) + WEIGHT_DECAY * weight_here
    inner = weight_here - INNER_RATE * update
    return (inner, first_new, second_new, projected)

def reference(activations, cotangent, weight, first_moment, second_moment, anchor, outer_momentum, fragment_rows):
    inner, first_out, second_out, projected = lax.map(replica_step, (activations, cotangent, weight, first_moment, second_moment))
    pseudo_grad = lax.optimization_barrier(jnp.sum(anchor[None] - weight, axis=0)) / N_REPLICA
    in_fragment = (fragment_rows == 1)[:, None]
    momentum_new = OUTER_MU * outer_momentum + pseudo_grad
    anchor_new = anchor - OUTER_RATE * (pseudo_grad + OUTER_MU * momentum_new)
    momentum_out = jnp.where(in_fragment, momentum_new, outer_momentum)
    anchor_out = jnp.where(in_fragment, anchor_new, anchor)
    merged = (1.0 - MIX_SHARE) * inner + MIX_SHARE * anchor_out[None]
    weight_out = jnp.where(in_fragment[None], merged, inner)
    return (weight_out, first_out, second_out, anchor_out, momentum_out, projected)
```

```python
import jax
import jax.numpy as jnp
from jax import lax
from jax.experimental import pallas as pl
from jax.experimental.pallas import tpu as pltpu
from jax.sharding import PartitionSpec as P

D = 4096
C = 512
STEP = 20
NX = 4
NY = 8
NH = 4
ROWS = 256
TOK = 192
COLS = 16

FIRST_DECAY = 0.9
SECOND_DECAY = 0.95
ADAM_EPS = 1e-08
INNER_RATE = 0.02
WEIGHT_DECAY = 0.1
OUTER_RATE = 0.7
OUTER_MU = 0.9
MIX_SHARE = 0.5

BF = jnp.bfloat16
F32 = jnp.float32
MESH = pl.DeviceIdType.MESH


def kernel(
    act,
    cot,
    w_hbm,
    anchor,
    mom,
    frag,
    g_out,
    y_out,
    a_out,
    anchor_out,
    mom_out,
    w32,
    xq,
    cq,
    wq,
    acc,
    g_send,
    g_opp,
    g_sum,
    g_dir,
    y_send,
    y_sib,
    y_mid,
    y_far,
    wt,
    ybuf,
    s32,
    s16,
    zbuf,
    at,
    local_sem,
    x_send,
    x_recv,
    c_send,
    c_recv,
    w_send,
    w_recv,
    gs_send,
    gs_recv,
    ys_send,
    ys_recv,
    r_send,
    r_recv,
    h_send,
    h_recv,
    b_send,
    b_recv,
    a_send,
    a_recv,
):
    rep = lax.axis_index("replica")
    ten = lax.axis_index("tensor")
    y, h = rep // NH, rep % NH
    x, q = ten // 4, ten % 4
    z, c = q // 2, q % 2
    s = 1 - 2 * c

    def quad(zz, cc):
        return zz * 2 + cc

    others = ((z, 1 - c), (1 - z, c), (1 - z, 1 - c))
    q_sib, q_far, q_diag = (quad(*o) for o in others)
    ahead = (x + s + NX) % NX
    behind = (x - s + NX) % NX
    sib = (rep, x * 4 + q_sib)
    far = (rep, x * 4 + q_far)
    diag = (rep, x * 4 + q_diag)
    dev_ahead = (rep, ahead * 4 + q)
    dev_behind = (rep, behind * 4 + q)

    def y_dev(d):
        return (((y + d) % NY) * NH + h, ten)

    def h_dev(d):
        return (y * NH + (h + d) % NH, ten)

    peers = [sib, far, diag, dev_ahead, dev_behind]
    peers += [y_dev(d) for d in range(1, NY)] + [h_dev(d) for d in range(1, NH)]

    def remote(src, dst, send, recv, dev):
        return pltpu.make_async_remote_copy(
            src_ref=src, dst_ref=dst, send_sem=send, recv_sem=recv, device_id=dev, device_id_type=MESH
        )

    def rows(i, n=TOK):
        return pl.ds(pl.multiple_of(i * n, n if n % 16 else 16), n)

    def rows_tok(i):
        return pl.ds(pl.multiple_of(i * TOK, TOK), TOK)

    def x_block(cc, qq, j):
        ss = 1 - 2 * cc
        shift = (2, ss + NX, NX - ss, 0)[j]
        k = ((x + shift) % NX) * 4 + qq
        return act.at[:, pl.ds(pl.multiple_of(k * ROWS, ROWS), ROWS)]

    w_copy = pltpu.make_async_copy(w_hbm, w32, local_sem.at[0])
    w_copy.start()
    c_copy = pltpu.make_async_copy(cot, cq.at[rows_tok(q)], local_sem.at[1])
    c_copy.start()
    x_copies = [
        pltpu.make_async_copy(x_block(c, q, j), xq.at[j, rows_tok(q)], local_sem.at[2 + j]) for j in range(4)
    ]
    for copy in x_copies:
        copy.start()

    barrier = pltpu.get_barrier_semaphore()
    for dev in peers:
        pl.semaphore_signal(barrier, inc=1, device_id=dev, device_id_type=MESH)
    pl.semaphore_wait(barrier, len(peers))

    sends = []

    def start(copy):
        copy.start()
        sends.append(copy)
        return copy

    start(remote(cot, cq.at[rows_tok(q)], c_send.at[1], c_recv.at[1], far))
    start(remote(cot, cq.at[rows_tok(q)], c_send.at[0], c_recv.at[0], sib))
    for j in range(4):
        for e, (dev, (zz, cc)) in ((1, (far, others[1])), (2, (diag, others[2])), (0, (sib, others[0]))):
            start(
                remote(
                    x_block(cc, quad(zz, cc), j), xq.at[j, rows_tok(q)], x_send.at[j, e], x_recv.at[j, e], dev
                )
            )

    def x_wait(j):
        x_copies[j].wait()
        for e, qq in enumerate((q_sib, q_far, q_diag)):
            remote(act.at[:, pl.ds(0, ROWS)], xq.at[j, rows_tok(qq)], x_send.at[j, e], x_recv.at[j, e], sib).wait_recv()

    w_copy.wait()
    wq[3] = w32[...].astype(BF)
    start(remote(wq.at[3], wq.at[2], w_send.at[0], w_recv.at[2], dev_ahead))
    start(remote(wq.at[3], wq.at[1], w_send.at[1], w_recv.at[1], dev_behind))

    wt[...] = w32[...].T.astype(BF)
    for d in range(1, NY):
        to = (y + d) % NY
        start(remote(wt.at[pl.ds(pl.multiple_of(to * 64, 64), 64)], ybuf.at[d], r_send.at[d], r_recv.at[d], y_dev(d)))

    remote(cot, cq.at[rows_tok(q_far)], c_send.at[1], c_recv.at[1], far).wait_recv()
    start(remote(cq.at[rows_tok(q_far)], cq.at[rows_tok(q_far)], c_send.at[2], c_recv.at[2], sib))
    remote(wq.at[3], wq.at[2], w_send.at[0], w_recv.at[2], dev_ahead).wait_recv()
    start(remote(wq.at[2], wq.at[0], w_send.at[2], w_recv.at[0], dev_ahead))

    total = wt[pl.ds(pl.multiple_of(y * 64, 64), 64), :].astype(F32)
    for d in range(1, NY):
        remote(wt.at[pl.ds(0, 64)], ybuf.at[d], r_send.at[d], r_recv.at[d], y_dev(d)).wait_recv()
        total = total + ybuf[d].astype(F32)
    s32[...] = total
    s16[...] = total.astype(BF)
    for d in range(1, NH):
        to = (h + d) % NH
        start(remote(s16.at[pl.ds(pl.multiple_of(to * COLS, COLS), COLS)], zbuf.at[d], h_send.at[d], h_recv.at[d], h_dev(d)))

    remote(cot, cq.at[rows_tok(q_sib)], c_send.at[0], c_recv.at[0], sib).wait_recv()
    remote(cot, cq.at[rows_tok(q_diag)], c_send.at[2], c_recv.at[2], sib).wait_recv()
    c_copy.wait()

    def grad(j):
        return lax.dot_general(xq[j], cq[...], (((0,), (0,)), ((), ())), preferred_element_type=F32)

    def project(j):
        return jnp.dot(xq[j], wq[j], preferred_element_type=F32)

    x_wait(0)
    g_send[0] = grad(0).astype(BF)
    start(remote(g_send.at[0], g_opp, gs_send.at[0], gs_recv.at[0], dev_ahead))

    mine = pl.ds(pl.multiple_of(h * COLS, COLS), COLS)
    total = s32[mine, :]
    for d in range(1, NH):
        remote(s16.at[pl.ds(0, COLS)], zbuf.at[d], h_send.at[d], h_recv.at[d], h_dev(d)).wait_recv()
        total = total + zbuf[d].astype(F32)
    old = anchor[...]
    old_mom = mom[...]
    inside = frag[...] == 1
    pseudo = old - total * (1.0 / (NY * NH))
    new_mom = OUTER_MU * old_mom + pseudo
    new_anchor = jnp.where(inside, old - OUTER_RATE * (pseudo + OUTER_MU * new_mom), old)
    anchor_out[...] = new_anchor
    mom_out[...] = jnp.where(inside, new_mom, old_mom)
    my_rows = pl.ds(pl.multiple_of(rep * COLS, COLS), COLS)
    at[my_rows, :] = new_anchor.astype(BF)
    for d in range(1, NH):
        start(remote(at.at[my_rows], at.at[my_rows], b_send.at[d], b_recv.at[d], h_dev(d)))

    remote(wq.at[2], wq.at[0], w_send.at[2], w_recv.at[0], dev_ahead).wait_recv()
    acc[...] = project(0)

    x_wait(1)
    g = grad(1)
    remote(g_send.at[0], g_opp, gs_send.at[0], gs_recv.at[0], dev_ahead).wait_recv()
    g_send[1] = (g + g_opp[...].astype(F32)).astype(BF)
    start(remote(g_send.at[1], g_sum, gs_send.at[1], gs_recv.at[1], dev_ahead))

    for d in range(1, NH):
        src = pl.ds(pl.multiple_of((y * NH + (h - d + NH) % NH) * COLS, COLS), COLS)
        remote(at.at[src], at.at[src], b_send.at[d], b_recv.at[d], h_dev(d)).wait_recv()
    y_rows = pl.ds(pl.multiple_of(y * 64, 64), 64)
    for d in range(1, NY):
        start(remote(at.at[y_rows], at.at[y_rows], a_send.at[d], a_recv.at[d], y_dev(d)))

    remote(wq.at[3], wq.at[1], w_send.at[1], w_recv.at[1], dev_behind).wait_recv()
    acc[...] += project(1)

    x_wait(2)
    g_send[2] = grad(2).astype(BF)
    start(remote(g_send.at[2], g_dir, gs_send.at[2], gs_recv.at[2], dev_behind))
    acc[...] += project(2)

    for d in range(1, NY):
        src = pl.ds(pl.multiple_of(((y - d + NY) % NY) * 64, 64), 64)
        remote(at.at[src], at.at[src], a_send.at[d], a_recv.at[d], y_dev(d)).wait_recv()
    a_out[...] = at[...].astype(F32).T.astype(BF)

    x_wait(3)
    acc[...] += project(3)
    y_send[0] = acc[rows_tok(q_diag), :].astype(BF)
    start(remote(y_send.at[0], y_mid, ys_send.at[0], ys_recv.at[0], sib))
    y_send[1] = acc[rows_tok(q_sib), :].astype(BF)
    start(remote(y_send.at[1], y_sib, ys_send.at[1], ys_recv.at[1], sib))
    g = grad(3)
    remote(y_send.at[0], y_mid, ys_send.at[0], ys_recv.at[0], sib).wait_recv()
    y_send[2] = (acc[rows_tok(q_far), :] + y_mid[...].astype(F32)).astype(BF)
    start(remote(y_send.at[2], y_far, ys_send.at[2], ys_recv.at[2], far))
    remote(g_send.at[1], g_sum, gs_send.at[1], gs_recv.at[1], dev_ahead).wait_recv()
    g = g + g_sum[...].astype(F32)
    remote(g_send.at[2], g_dir, gs_send.at[2], gs_recv.at[2], dev_behind).wait_recv()
    g_out[...] = g + g_dir[...].astype(F32)

    remote(y_send.at[1], y_sib, ys_send.at[1], ys_recv.at[1], sib).wait_recv()
    total = acc[rows_tok(q), :] + y_sib[...].astype(F32)
    remote(y_send.at[2], y_far, ys_send.at[2], ys_recv.at[2], far).wait_recv()
    y_out[...] = ((total + y_far[...].astype(F32)) * D ** (-0.5)).astype(BF)

    for copy in sends:
        copy.wait_send()


def body(
    activations,
    cotangent,
    weight,
    first_moment,
    second_moment,
    anchor,
    outer_momentum,
    fragment_rows,
):
    weight_here = weight[0]
    vmem = pl.BlockSpec(memory_space=pltpu.VMEM)
    hbm = pl.BlockSpec(memory_space=pl.ANY)
    dma = pltpu.SemaphoreType.DMA
    gradient, projected, anchor_full, anchor_new, momentum_new = pl.pallas_call(
        kernel,
        out_shape=(
            jax.ShapeDtypeStruct((ROWS, C), F32),
            jax.ShapeDtypeStruct((TOK, C), BF),
            jax.ShapeDtypeStruct((ROWS, C), BF),
            jax.ShapeDtypeStruct((COLS, ROWS), F32),
            jax.ShapeDtypeStruct((COLS, ROWS), F32),
        ),
        in_specs=[hbm, hbm, hbm, vmem, vmem, vmem],
        out_specs=[vmem] * 5,
        scratch_shapes=[
            pltpu.VMEM((ROWS, C), F32),
            pltpu.VMEM((4, 4 * TOK, ROWS), BF),
            pltpu.VMEM((4 * TOK, C), BF),
            pltpu.VMEM((4, ROWS, C), BF),
            pltpu.VMEM((4 * TOK, C), F32),
            pltpu.VMEM((3, ROWS, C), BF),
            pltpu.VMEM((ROWS, C), BF),
            pltpu.VMEM((ROWS, C), BF),
            pltpu.VMEM((ROWS, C), BF),
            pltpu.VMEM((3, TOK, C), BF),
            pltpu.VMEM((TOK, C), BF),
            pltpu.VMEM((TOK, C), BF),
            pltpu.VMEM((TOK, C), BF),
            pltpu.VMEM((C, ROWS), BF),
            pltpu.VMEM((NY, 64, ROWS), BF),
            pltpu.VMEM((64, ROWS), F32),
            pltpu.VMEM((64, ROWS), BF),
            pltpu.VMEM((NH, COLS, ROWS), BF),
            pltpu.VMEM((C, ROWS), BF),
            dma((6,)),
            dma((4, 3)),
            dma((4, 3)),
            dma((3,)),
            dma((3,)),
            dma((3,)),
            dma((3,)),
            dma((3,)),
            dma((3,)),
            dma((3,)),
            dma((3,)),
            dma((NY,)),
            dma((NY,)),
            dma((NH,)),
            dma((NH,)),
            dma((NH,)),
            dma((NH,)),
            dma((NY,)),
            dma((NY,)),
        ],
        compiler_params=pltpu.CompilerParams(
            collective_id=0, has_side_effects=True, vmem_limit_bytes=32 * 1024 * 1024
        ),
        name="exchange",
    )(
        activations[0],
        cotangent[0],
        weight_here,
        anchor.T,
        outer_momentum.T,
        fragment_rows[None, :],
    )
    gradient = gradient * D ** (-0.5)
    first_new = FIRST_DECAY * first_moment[0] + (1.0 - FIRST_DECAY) * gradient
    second_new = SECOND_DECAY * second_moment[0] + (1.0 - SECOND_DECAY) * gradient * gradient
    first_hat = first_new / (1.0 - FIRST_DECAY**STEP)
    second_hat = second_new / (1.0 - SECOND_DECAY**STEP)
    update = first_hat / (jnp.sqrt(second_hat) + ADAM_EPS) + WEIGHT_DECAY * weight_here
    inner = weight_here - INNER_RATE * update
    in_fragment = (fragment_rows == 1)[:, None]
    merged = (1.0 - MIX_SHARE) * inner + MIX_SHARE * anchor_full.astype(F32)
    weight_out = jnp.where(in_fragment, merged, inner)
    return (
        weight_out[None],
        first_new[None],
        second_new[None],
        anchor_new.T,
        momentum_new.T,
        projected[None],
    )


def solution(mesh):
    return jax.shard_map(
        body,
        mesh=mesh,
        in_specs=(
            P("replica", "tensor", None),
            P("replica", "tensor", None),
            P("replica", "tensor", None),
            P("replica", "tensor", None),
            P("replica", "tensor", None),
            P("tensor", "replica"),
            P("tensor", "replica"),
            P("tensor"),
        ),
        out_specs=(
            P("replica", "tensor", None),
            P("replica", "tensor", None),
            P("replica", "tensor", None),
            P("tensor", "replica"),
            P("tensor", "replica"),
            P("replica", "tensor", None),
        ),
        check_vma=False,
    )
```

```python
import jax
import jax.numpy as jnp
from jax import lax
from jax.experimental import pallas as pl
from jax.experimental.pallas import tpu as pltpu
from jax.sharding import PartitionSpec as P

D = 4096
C = 512
STEP = 20
NX = 4
NY = 8
NH = 4
ROWS = 256
TOK = 192
HALF = TOK // 2
COLS = 16
BAND = NH * COLS
SCALE = D ** (-0.5)

FIRST_DECAY = 0.9
SECOND_DECAY = 0.95
ADAM_EPS = 1e-08
INNER_RATE = 0.02
WEIGHT_DECAY = 0.1
OUTER_RATE = 0.7
OUTER_MU = 0.9
MIX_SHARE = 0.5

BF = jnp.bfloat16
F32 = jnp.float32
MESH = pl.DeviceIdType.MESH
AHEAD = 3


def exchange(
    act,
    cot,
    weight,
    anchor,
    mom,
    frag,
    first,
    second,
    w_out,
    first_out,
    second_out,
    anchor_out,
    mom_out,
    y_out,
    w32,
    f32,
    v32,
    old_anchor,
    old_mom,
    frag_v,
    xq,
    cq,
    wq,
    acc,
    g_send,
    g_opp,
    g_sum,
    g_dir,
    g_res,
    ym_out,
    ym_in,
    ys_out,
    ys_in,
    yf_out,
    yf_in,
    y_res,
    wt,
    ybuf,
    s32,
    s16,
    zbuf,
    at,
    a_res,
    m_res,
    new_anchor,
    new_mom,
    local_sem,
    out_sem,
    x_send,
    x_recv,
    c_send,
    c_recv,
    w_send,
    w_recv,
    gs_send,
    gs_recv,
    ym_send,
    ym_recv,
    ys_send,
    ys_recv,
    yf_send,
    yf_recv,
    r_send,
    r_recv,
    h_send,
    h_recv,
    b_send,
    b_recv,
    a_send,
    a_recv,
):
    rep = lax.axis_index("replica")
    ten = lax.axis_index("tensor")
    y, h = rep // NH, rep % NH
    x, q = ten // 4, ten % 4
    z, c = q // 2, q % 2
    s = 1 - 2 * c

    others = ((z, 1 - c), (1 - z, c), (1 - z, 1 - c))
    q_sib, q_far, q_diag = (zz * 2 + cc for zz, cc in others)
    ahead = (x + s + NX) % NX
    behind = (x - s + NX) % NX
    sib = (rep, x * 4 + q_sib)
    far = (rep, x * 4 + q_far)
    diag = (rep, x * 4 + q_diag)
    dev_ahead = (rep, ahead * 4 + q)
    dev_behind = (rep, behind * 4 + q)

    def y_dev(d):
        return (((y + d) % NY) * NH + h, ten)

    def h_dev(d):
        return (y * NH + (h + d) % NH, ten)

    peers = [sib, far, diag, dev_ahead, dev_behind]
    peers += [y_dev(d) for d in range(1, NY)] + [h_dev(d) for d in range(1, NH)]
    barrier = pltpu.get_barrier_semaphore()
    for dev in peers:
        pl.semaphore_signal(barrier, inc=1, device_id=dev, device_id_type=MESH)

    def remote(src, dst, send, recv, dev):
        return pltpu.make_async_remote_copy(
            src_ref=src, dst_ref=dst, send_sem=send, recv_sem=recv, device_id=dev, device_id_type=MESH
        )

    def part(i, n):
        return pl.ds(pl.multiple_of(i * n, n), n)

    def halves(qq, k):
        return pl.ds(pl.multiple_of(qq * TOK + k * HALF, HALF), HALF)

    def x_cols(cc, qq, j):
        ss = 1 - 2 * cc
        shift = (2, ss + NX, NX - ss, 0)[j]
        return part(((x + shift) % NX) * 4 + qq, ROWS)

    def local(src, dst, sem):
        copy = pltpu.make_async_copy(src, dst, sem)
        copy.start()
        return copy

    w_copy = local(weight, w32, local_sem.at[0])
    c_copy = local(cot, cq.at[part(q, TOK)], local_sem.at[1])
    x_copies = [local(act.at[:, x_cols(c, q, j)], xq.at[j, part(q, TOK)], local_sem.at[2 + j]) for j in range(4)]
    small_copies = [
        local(anchor, old_anchor, local_sem.at[6]),
        local(mom, old_mom, local_sem.at[7]),
        local(frag, frag_v, local_sem.at[8]),
    ]
    moment_copies = [local(first, f32, local_sem.at[9]), local(second, v32, local_sem.at[10])]

    w_copy.wait()
    wt[...] = w32[...].T.astype(BF)
    wq[3] = w32[...].astype(BF)
    for copy in small_copies:
        copy.wait()
    m_res[...] = jnp.broadcast_to((frag_v[...] == 1).astype(F32), (128, ROWS)).T

    pl.semaphore_wait(barrier, len(peers))

    sends = []

    def start(copy):
        copy.start()
        sends.append(copy)
        return copy

    stage_r = {}
    for d in range(1, NY):
        stage_r[d] = start(
            remote(wt.at[part((y + d) % NY, BAND)], ybuf.at[d], r_send.at[d], r_recv.at[d], y_dev(d))
        )

    w_ahead = start(remote(wq.at[3], wq.at[2], w_send.at[0], w_recv.at[0], dev_ahead))
    w_behind = start(remote(wq.at[3], wq.at[1], w_send.at[1], w_recv.at[1], dev_behind))
    start(remote(cot, cq.at[part(q, TOK)], c_send.at[1], c_recv.at[1], far))
    start(remote(cot, cq.at[part(q, TOK)], c_send.at[0], c_recv.at[0], sib))
    targets = ((1, far, others[1]), (2, diag, others[2]), (0, sib, others[0]))

    def x_issue(u):
        j, k = u // 2, u % 2
        for e, dev, (zz, cc) in targets:
            src = act.at[pl.ds(k * HALF, HALF), x_cols(cc, zz * 2 + cc, j)]
            start(remote(src, xq.at[j, halves(q, k)], x_send.at[u, e], x_recv.at[u, e], dev))

    def x_wait(u):
        j, k = u // 2, u % 2
        if k == 0:
            x_copies[j].wait()
        for e, qq in enumerate((q_sib, q_far, q_diag)):
            src = act.at[pl.ds(0, HALF), pl.ds(0, ROWS)]
            remote(src, xq.at[j, halves(qq, k)], x_send.at[u, e], x_recv.at[u, e], sib).wait_recv()
        if u + AHEAD < 8:
            x_issue(u + AHEAD)

    for u in range(AHEAD):
        x_issue(u)

    w_ahead.wait_recv()
    w_pass = start(remote(wq.at[2], wq.at[0], w_send.at[2], w_recv.at[2], dev_ahead))
    remote(cot, cq.at[part(q_far, TOK)], c_send.at[1], c_recv.at[1], far).wait_recv()
    start(remote(cq.at[part(q_far, TOK)], cq.at[part(q_far, TOK)], c_send.at[2], c_recv.at[2], sib))

    def grad(j):
        return lax.dot_general(xq[j], cq[...], (((0,), (0,)), ((), ())), preferred_element_type=F32)

    def project(j):
        return jnp.dot(xq[j], wq[j], preferred_element_type=F32)

    x_wait(0)

    total = wt[part(y, BAND), :].astype(F32)
    for d in range(1, NY):
        stage_r[d].wait_recv()
        total = total + ybuf[d].astype(F32)
    s32[...] = total
    s16[...] = total.astype(BF)
    stage_h = {}
    for d in range(1, NH):
        stage_h[d] = start(remote(s16.at[part((h + d) % NH, COLS)], zbuf.at[d], h_send.at[d], h_recv.at[d], h_dev(d)))

    x_wait(1)
    remote(cot, cq.at[part(q_sib, TOK)], c_send.at[0], c_recv.at[0], sib).wait_recv()
    remote(cot, cq.at[part(q_diag, TOK)], c_send.at[2], c_recv.at[2], sib).wait_recv()
    c_copy.wait()
    g_send[0] = grad(0).astype(BF)
    to_opp = start(remote(g_send.at[0], g_opp, gs_send.at[0], gs_recv.at[0], dev_ahead))

    mine = part(h, COLS)
    total = s32[mine, :]
    for d in range(1, NH):
        stage_h[d].wait_recv()
        total = total + zbuf[d].astype(F32)
    inside = frag_v[...] == 1
    pseudo = old_anchor[...] - total * (1.0 / (NY * NH))
    momentum = OUTER_MU * old_mom[...] + pseudo
    moved = old_anchor[...] - OUTER_RATE * (pseudo + OUTER_MU * momentum)
    at[part(rep, COLS), :] = jnp.where(inside, MIX_SHARE * moved, 0.0).astype(BF)
    for d in range(1, NH):
        start(remote(at.at[part(rep, COLS)], at.at[part(rep, COLS)], b_send.at[d], b_recv.at[d], h_dev(d)))
    new_anchor[...] = jnp.where(inside, moved, old_anchor[...])
    new_mom[...] = jnp.where(inside, momentum, old_mom[...])
    outs = [local(new_anchor, anchor_out, out_sem.at[0]), local(new_mom, mom_out, out_sem.at[1])]

    x_wait(2)
    w_pass.wait_recv()
    acc[...] = project(0)

    x_wait(3)
    g = grad(1)
    to_opp.wait_recv()
    g_send[1] = (g + g_opp[...].astype(F32)).astype(BF)
    to_ahead = start(remote(g_send.at[1], g_sum, gs_send.at[1], gs_recv.at[1], dev_ahead))

    for d in range(1, NH):
        theirs = part(y * NH + (h - d + NH) % NH, COLS)
        remote(at.at[theirs], at.at[theirs], b_send.at[d], b_recv.at[d], h_dev(d)).wait_recv()
    for d in range(1, NY):
        start(remote(at.at[part(y, BAND)], at.at[part(y, BAND)], a_send.at[d], a_recv.at[d], y_dev(d)))

    x_wait(4)
    w_behind.wait_recv()
    acc[...] += project(1)

    x_wait(5)
    g_send[2] = grad(2).astype(BF)
    to_behind = start(remote(g_send.at[2], g_dir, gs_send.at[2], gs_recv.at[2], dev_behind))
    acc[...] += project(2)

    def last(qq, k):
        return acc[halves(qq, k), :] + jnp.dot(xq[3, halves(qq, k), :], wq[3], preferred_element_type=F32)

    mids, sibs, fars = {}, {}, {}
    for k in range(2):
        x_wait(6 + k)
        ym_out[k] = last(q_diag, k).astype(BF)
        mids[k] = start(remote(ym_out.at[k], ym_in.at[k], ym_send.at[k], ym_recv.at[k], sib))
        ys_out[k] = last(q_sib, k).astype(BF)
        sibs[k] = start(remote(ys_out.at[k], ys_in.at[k], ys_send.at[k], ys_recv.at[k], sib))
        beyond = last(q_far, k)
        acc[halves(q, k), :] = last(q, k)
        mids[k].wait_recv()
        yf_out[k] = (beyond + ym_in[k].astype(F32)).astype(BF)
        fars[k] = start(remote(yf_out.at[k], yf_in.at[k], yf_send.at[k], yf_recv.at[k], far))

    g_res[...] = grad(3)
    for d in range(1, NY):
        theirs = part((y - d + NY) % NY, BAND)
        remote(at.at[theirs], at.at[theirs], a_send.at[d], a_recv.at[d], y_dev(d)).wait_recv()
    a_res[...] = at[...].astype(F32).T
    to_ahead.wait_recv()
    to_behind.wait_recv()
    for copy in moment_copies:
        copy.wait()

    def inner_step(i, carry):
        r = part(i, 32)
        gradient = (g_res[r, :] + g_sum[r, :].astype(F32) + g_dir[r, :].astype(F32)) * SCALE
        moment = FIRST_DECAY * f32[r, :] + (1.0 - FIRST_DECAY) * gradient
        square = SECOND_DECAY * v32[r, :] + (1.0 - SECOND_DECAY) * gradient * gradient
        f32[r, :] = moment
        v32[r, :] = square
        first_hat = moment / (1.0 - FIRST_DECAY**STEP)
        second_hat = square / (1.0 - SECOND_DECAY**STEP)
        update = first_hat / (jnp.sqrt(second_hat) + ADAM_EPS) + WEIGHT_DECAY * w32[r, :]
        inner = w32[r, :] - INNER_RATE * update
        share = 1.0 - MIX_SHARE * m_res[r, :][:, :1]
        w32[r, :] = inner * share + a_res[r, :]
        return carry

    lax.fori_loop(0, ROWS // 32, inner_step, 0)
    outs += [
        local(w32, w_out, out_sem.at[2]),
        local(f32, first_out, out_sem.at[3]),
        local(v32, second_out, out_sem.at[4]),
    ]

    for k in range(2):
        sibs[k].wait_recv()
        fars[k].wait_recv()
        total = acc[halves(q, k), :] + ys_in[k].astype(F32) + yf_in[k].astype(F32)
        y_res[pl.ds(k * HALF, HALF), :] = (total * SCALE).astype(BF)
    outs.append(local(y_res, y_out, out_sem.at[5]))

    for copy in sends:
        copy.wait_send()
    for copy in outs:
        copy.wait()


def finish(*refs):
    sources, results, held, in_sem, out_sem = refs[:6], refs[6:12], refs[12:18], refs[18], refs[19]
    comes = [pltpu.make_async_copy(a, b, in_sem.at[i]) for i, (a, b) in enumerate(zip(sources, held))]
    goes = [pltpu.make_async_copy(a, b, out_sem.at[i]) for i, (a, b) in enumerate(zip(held, results))]
    for copy in comes:
        copy.start()
    for before, after in zip(comes, goes):
        before.wait()
        after.start()
    for copy in goes:
        copy.wait()


def body(
    activations,
    cotangent,
    weight,
    first_moment,
    second_moment,
    anchor,
    outer_momentum,
    fragment_rows,
):
    hbm = pl.BlockSpec(memory_space=pltpu.HBM)
    free = pl.BlockSpec(memory_space=pl.ANY)
    dma = pltpu.SemaphoreType.DMA
    vm = pltpu.VMEM
    shape = jax.ShapeDtypeStruct
    out_shape = (
        shape((ROWS, C), F32),
        shape((ROWS, C), F32),
        shape((ROWS, C), F32),
        shape((COLS, ROWS), F32),
        shape((COLS, ROWS), F32),
        shape((TOK, C), BF),
    )
    results = pl.pallas_call(
        exchange,
        out_shape=out_shape,
        in_specs=[hbm] * 8,
        out_specs=[free] * 6,
        scratch_shapes=[
            vm((ROWS, C), F32),
            vm((ROWS, C), F32),
            vm((ROWS, C), F32),
            vm((COLS, ROWS), F32),
            vm((COLS, ROWS), F32),
            vm((1, ROWS), jnp.int32),
            vm((4, 4 * TOK, ROWS), BF),
            vm((4 * TOK, C), BF),
            vm((4, ROWS, C), BF),
            vm((4 * TOK, C), F32),
            vm((3, ROWS, C), BF),
            vm((ROWS, C), BF),
            vm((ROWS, C), BF),
            vm((ROWS, C), BF),
            vm((ROWS, C), F32),
            vm((2, HALF, C), BF),
            vm((2, HALF, C), BF),
            vm((2, HALF, C), BF),
            vm((2, HALF, C), BF),
            vm((2, HALF, C), BF),
            vm((2, HALF, C), BF),
            vm((TOK, C), BF),
            vm((C, ROWS), BF),
            vm((NY, BAND, ROWS), BF),
            vm((BAND, ROWS), F32),
            vm((BAND, ROWS), BF),
            vm((NH, COLS, ROWS), BF),
            vm((C, ROWS), BF),
            vm((ROWS, C), F32),
            vm((ROWS, 128), F32),
            vm((COLS, ROWS), F32),
            vm((COLS, ROWS), F32),
            dma((11,)),
            dma((6,)),
            dma((8, 3)),
            dma((8, 3)),
            dma((3,)),
            dma((3,)),
            dma((3,)),
            dma((3,)),
            dma((3,)),
            dma((3,)),
            dma((2,)),
            dma((2,)),
            dma((2,)),
            dma((2,)),
            dma((2,)),
            dma((2,)),
            dma((NY,)),
            dma((NY,)),
            dma((NH,)),
            dma((NH,)),
            dma((NH,)),
            dma((NH,)),
            dma((NY,)),
            dma((NY,)),
        ],
        compiler_params=pltpu.CompilerParams(
            collective_id=0, has_side_effects=True, vmem_limit_bytes=60 * 1024 * 1024
        ),
        name="exchange",
    )(
        activations[0],
        cotangent[0],
        weight[0],
        anchor.T,
        outer_momentum.T,
        fragment_rows[None, :],
        first_moment[0],
        second_moment[0],
    )

    weight_out, first_new, second_new, anchor_new, momentum_new, projected = pl.pallas_call(
        finish,
        out_shape=out_shape,
        in_specs=[hbm] * 6,
        out_specs=[hbm] * 6,
        scratch_shapes=[vm(a.shape, a.dtype) for a in out_shape] + [dma((6,))] * 2,
        compiler_params=pltpu.CompilerParams(vmem_limit_bytes=60 * 1024 * 1024),
        name="finish",
    )(*results)
    return (
        weight_out[None],
        first_new[None],
        second_new[None],
        anchor_new.T,
        momentum_new.T,
        projected[None],
    )


def solution(mesh):
    return jax.shard_map(
        body,
        mesh=mesh,
        in_specs=(
            P("replica", "tensor", None),
            P("replica", "tensor", None),
            P("replica", "tensor", None),
            P("replica", "tensor", None),
            P("replica", "tensor", None),
            P("tensor", "replica"),
            P("tensor", "replica"),
            P("tensor"),
        ),
        out_specs=(
            P("replica", "tensor", None),
            P("replica", "tensor", None),
            P("replica", "tensor", None),
            P("tensor", "replica"),
            P("tensor", "replica"),
            P("replica", "tensor", None),
        ),
        check_vma=False,
    )
```

```python
import jax
import jax.numpy as jnp
from jax import lax
from jax.experimental import pallas as pl
from jax.experimental.pallas import tpu as pltpu
from jax.sharding import PartitionSpec as P

D = 4096
C = 512
STEP = 20
NX = 4
NY = 8
NH = 4
ROWS = 256
TOK = 192
CUT = 96
UNITS = TOK // CUT
COLS = 16
BAND = NH * COLS
SCALE = D ** (-0.5)

FIRST_DECAY = 0.9
SECOND_DECAY = 0.95
ADAM_EPS = 1e-08
INNER_RATE = 0.02
WEIGHT_DECAY = 0.1
OUTER_RATE = 0.7
OUTER_MU = 0.9
MIX_SHARE = 0.5

BF = jnp.bfloat16
F32 = jnp.float32
MESH = pl.DeviceIdType.MESH
AHEAD = 2
PLACES = (0, 2, 4)
PARTS = ((0, 96), (96, 96))


def exchange(
    act,
    cot,
    weight,
    anchor,
    mom,
    frag,
    first,
    second,
    w_out,
    first_out,
    second_out,
    anchor_out,
    mom_out,
    y_out,
    w32,
    f32,
    v32,
    old_anchor,
    old_mom,
    frag_v,
    xq,
    cq,
    wq,
    acc,
    g_send,
    g_opp,
    g_sum,
    g_dir,
    g_res,
    ym_out,
    ym_in,
    ys_out,
    ys_in,
    yf_out,
    yf_in,
    wt,
    ybuf,
    s32,
    s16,
    zbuf,
    at,
    m_res,
    local_sem,
    x_send,
    x_recv,
    c_send,
    c_recv,
    w_send,
    w_recv,
    gs_send,
    gs_recv,
    ym_send,
    ym_recv,
    ys_send,
    ys_recv,
    yf_send,
    yf_recv,
    r_send,
    r_recv,
    h_send,
    h_recv,
    b_send,
    b_recv,
    a_send,
    a_recv,
):
    rep = lax.axis_index("replica")
    ten = lax.axis_index("tensor")
    y, h = rep // NH, rep % NH
    x, z, c = ten // 4, (ten // 2) % 2, ten % 2
    pair = x // 2
    side = (x + pair) % 2
    place = pair + z * (3 - 2 * pair)
    q = side * 2 + c
    s = 1 - 2 * c

    def tensor_at(i, g, cc):
        zz = i // 2
        p = (i + zz) % 2
        return (g + p * (3 - 2 * g)) * 4 + zz * 2 + cc

    others = ((side, 1 - c), (1 - side, c), (1 - side, 1 - c))
    q_sib, q_far, q_diag = (g * 2 + cc for g, cc in others)
    sib, far, diag = ((rep, tensor_at(place, g, cc)) for g, cc in others)
    dev_ahead = (rep, tensor_at((place + s + NX) % NX, side, c))
    dev_behind = (rep, tensor_at((place - s + NX) % NX, side, c))

    def y_dev(d):
        return (((y + d) % NY) * NH + h, ten)

    def h_dev(d):
        return (y * NH + (h + d) % NH, ten)

    peers = [sib, far, diag, dev_ahead, dev_behind]
    peers += [y_dev(d) for d in range(1, NY)] + [h_dev(d) for d in range(1, NH)]
    y_order = (4, 3, 5, 2, 6, 1, 7)
    h_order = (2, 1, 3)
    barrier = pltpu.get_barrier_semaphore()
    for dev in peers:
        pl.semaphore_signal(barrier, inc=1, device_id=dev, device_id_type=MESH)

    def remote(src, dst, send, recv, dev):
        return pltpu.make_async_remote_copy(
            src_ref=src, dst_ref=dst, send_sem=send, recv_sem=recv, device_id=dev, device_id_type=MESH
        )

    def part(i, n):
        return pl.ds(pl.multiple_of(i * n, n), n)

    def tokens(qq, first_row, n):
        return pl.ds(pl.multiple_of(qq * TOK + first_row, 16), n)

    def x_cols(g, cc, j):
        ss = 1 - 2 * cc
        shift = (2, ss + NX, NX - ss, 0)[j]
        return part(tensor_at((place + shift) % NX, g, cc), ROWS)

    def local(src, dst, sem):
        copy = pltpu.make_async_copy(src, dst, sem)
        copy.start()
        return copy

    w_copy = local(weight, w32, local_sem.at[0])
    c_copy = local(cot, cq.at[part(q, TOK)], local_sem.at[1])
    x_copies = [local(act.at[:, x_cols(side, c, j)], xq.at[j, part(q, TOK)], local_sem.at[2 + j]) for j in range(4)]
    small_copies = [
        local(anchor, old_anchor, local_sem.at[6]),
        local(mom, old_mom, local_sem.at[7]),
        local(frag, frag_v, local_sem.at[8]),
    ]
    moment_copies = [local(first, f32, local_sem.at[9]), local(second, v32, local_sem.at[10])]

    pl.semaphore_wait(barrier, len(peers))

    sends = []

    def start(copy):
        copy.start()
        sends.append(copy)
        return copy

    targets = ((1, far, others[1]), (2, diag, others[2]), (0, sib, others[0]))

    def x_issue(u):
        j, k = u // UNITS, u % UNITS
        for e, dev, (g, cc) in targets:
            src = act.at[pl.ds(k * CUT, CUT), x_cols(g, cc, j)]
            start(remote(src, xq.at[j, tokens(q, k * CUT, CUT)], x_send.at[u, e], x_recv.at[u, e], dev))

    def x_wait(u):
        j, k = u // UNITS, u % UNITS
        if k == 0:
            x_copies[j].wait()
        for e, qq in enumerate((q_sib, q_far, q_diag)):
            src = act.at[pl.ds(0, CUT), pl.ds(0, ROWS)]
            dst = xq.at[j, tokens(qq, k * CUT, CUT)]
            remote(src, dst, x_send.at[u, e], x_recv.at[u, e], sib).wait_recv()
        if u + AHEAD < 4 * UNITS:
            x_issue(u + AHEAD)

    def x_half(i):
        for u in range(i * UNITS // 2, (i + 1) * UNITS // 2):
            x_wait(u)

    def send_features():
        start(remote(cot, cq.at[part(q, TOK)], c_send.at[1], c_recv.at[1], far))
        start(remote(cot, cq.at[part(q, TOK)], c_send.at[0], c_recv.at[0], sib))
        for u in range(AHEAD):
            x_issue(u)

    stage_r = {}

    def send_columns():
        wt[...] = w32[...].T.astype(BF)
        for d in y_order:
            src = wt.at[part((y + d) % NY, BAND)]
            stage_r[d] = start(remote(src, ybuf.at[d], r_send.at[d], r_recv.at[d], y_dev(d)))

    send_features()
    w_copy.wait()
    wq[3] = w32[...].astype(BF)
    w_ahead = start(remote(wq.at[3], wq.at[2], w_send.at[0], w_recv.at[0], dev_ahead))
    w_behind = start(remote(wq.at[3], wq.at[1], w_send.at[1], w_recv.at[1], dev_behind))
    send_columns()
    for copy in small_copies:
        copy.wait()
    m_res[...] = jnp.broadcast_to((frag_v[...] == 1).astype(F32), (128, ROWS)).T

    w_ahead.wait_recv()
    w_pass = start(remote(wq.at[2], wq.at[0], w_send.at[2], w_recv.at[2], dev_ahead))
    remote(cot, cq.at[part(q_far, TOK)], c_send.at[1], c_recv.at[1], far).wait_recv()
    start(remote(cq.at[part(q_far, TOK)], cq.at[part(q_far, TOK)], c_send.at[2], c_recv.at[2], sib))

    def grad(j):
        return lax.dot_general(xq[j], cq[...], (((0,), (0,)), ((), ())), preferred_element_type=F32)

    def project(j):
        return jnp.dot(xq[j], wq[j], preferred_element_type=F32)

    stage_h = {}

    def sum_y():
        total = wt[part(y, BAND), :].astype(F32)
        for d in y_order:
            stage_r[d].wait_recv()
            total = total + ybuf[d].astype(F32)
        s32[...] = total
        s16[...] = total.astype(BF)
        for d in h_order:
            src = s16.at[part((h + d) % NH, COLS)]
            stage_h[d] = start(remote(src, zbuf.at[d], h_send.at[d], h_recv.at[d], h_dev(d)))

    def outer_step():
        total = s32[part(h, COLS), :]
        for d in h_order:
            stage_h[d].wait_recv()
            total = total + zbuf[d].astype(F32)
        inside = frag_v[...] == 1
        pseudo = old_anchor[...] - total * (1.0 / (NY * NH))
        momentum = OUTER_MU * old_mom[...] + pseudo
        moved = old_anchor[...] - OUTER_RATE * (pseudo + OUTER_MU * momentum)
        own = part(rep, COLS)
        at[own, :] = jnp.where(inside, MIX_SHARE * moved, 0.0).astype(BF)
        for d in h_order:
            start(remote(at.at[own], at.at[own], b_send.at[d], b_recv.at[d], h_dev(d)))
        anchor_out[...] = jnp.where(inside, moved, old_anchor[...])
        mom_out[...] = jnp.where(inside, momentum, old_mom[...])

    def gather_y():
        for d in h_order:
            theirs = part(y * NH + (h - d + NH) % NH, COLS)
            remote(at.at[theirs], at.at[theirs], b_send.at[d], b_recv.at[d], h_dev(d)).wait_recv()
        for d in y_order:
            start(remote(at.at[part(y, BAND)], at.at[part(y, BAND)], a_send.at[d], a_recv.at[d], y_dev(d)))

    def outer(u):
        for place, stage in zip(PLACES, (sum_y, outer_step, gather_y)):
            if place == u:
                stage()

    x_half(0)
    outer(0)
    x_half(1)
    remote(cot, cq.at[part(q_sib, TOK)], c_send.at[0], c_recv.at[0], sib).wait_recv()
    remote(cot, cq.at[part(q_diag, TOK)], c_send.at[2], c_recv.at[2], sib).wait_recv()
    c_copy.wait()
    g_send[0] = grad(0).astype(BF)
    to_opp = start(remote(g_send.at[0], g_opp, gs_send.at[0], gs_recv.at[0], dev_ahead))
    outer(1)

    x_half(2)
    w_pass.wait_recv()
    acc[...] = project(0)
    outer(2)
    x_half(3)
    g = grad(1)
    to_opp.wait_recv()
    g_send[1] = (g + g_opp[...].astype(F32)).astype(BF)
    to_ahead = start(remote(g_send.at[1], g_sum, gs_send.at[1], gs_recv.at[1], dev_ahead))
    outer(3)

    x_half(4)
    w_behind.wait_recv()
    acc[...] += project(1)
    outer(4)
    x_half(5)
    g_send[2] = grad(2).astype(BF)
    to_behind = start(remote(g_send.at[2], g_dir, gs_send.at[2], gs_recv.at[2], dev_behind))
    acc[...] += project(2)
    outer(5)

    def last(qq, r, n):
        rows = tokens(qq, r, n)
        return acc[rows, :] + jnp.dot(xq[3, rows, :], wq[3], preferred_element_type=F32)

    mids, sibs, fars = {}, {}, {}
    for k, (r, n) in enumerate(PARTS):
        here = pl.ds(r, n)
        for u in range(r // CUT, (r + n) // CUT):
            x_wait(3 * UNITS + u)
        ym_out[here, :] = last(q_diag, r, n).astype(BF)
        mids[k] = start(remote(ym_out.at[here], ym_in.at[here], ym_send.at[k], ym_recv.at[k], sib))
        ys_out[here, :] = last(q_sib, r, n).astype(BF)
        sibs[k] = start(remote(ys_out.at[here], ys_in.at[here], ys_send.at[k], ys_recv.at[k], sib))
        beyond = last(q_far, r, n)
        own_rows = tokens(q, r, n)
        acc[own_rows, :] = last(q, r, n)
        mids[k].wait_recv()
        yf_out[here, :] = (beyond + ym_in[here, :].astype(F32)).astype(BF)
        fars[k] = start(remote(yf_out.at[here], yf_in.at[here], yf_send.at[k], yf_recv.at[k], far))
        outer(6 + k)

    g_res[...] = grad(3)
    to_ahead.wait_recv()
    to_behind.wait_recv()
    for copy in moment_copies:
        copy.wait()

    def inner_step(i, carry):
        r = part(i, 32)
        gradient = (g_res[r, :] + g_sum[r, :].astype(F32) + g_dir[r, :].astype(F32)) * SCALE
        moment = FIRST_DECAY * f32[r, :] + (1.0 - FIRST_DECAY) * gradient
        square = SECOND_DECAY * v32[r, :] + (1.0 - SECOND_DECAY) * gradient * gradient
        first_out[r, :] = moment
        second_out[r, :] = square
        first_hat = moment / (1.0 - FIRST_DECAY**STEP)
        second_hat = square / (1.0 - SECOND_DECAY**STEP)
        update = first_hat / (jnp.sqrt(second_hat) + ADAM_EPS) + WEIGHT_DECAY * w32[r, :]
        inner = w32[r, :] - INNER_RATE * update
        share = 1.0 - MIX_SHARE * m_res[r, :][:, :1]
        w32[r, :] = inner * share
        return carry

    lax.fori_loop(0, ROWS // 32, inner_step, 0)

    for k, (r, n) in enumerate(PARTS):
        here = pl.ds(r, n)
        sibs[k].wait_recv()
        fars[k].wait_recv()
        total = acc[tokens(q, r, n), :] + ys_in[here, :].astype(F32) + yf_in[here, :].astype(F32)
        y_out[here, :] = (total * SCALE).astype(BF)

    for d in y_order:
        theirs = part((y - d + NY) % NY, BAND)
        remote(at.at[theirs], at.at[theirs], a_send.at[d], a_recv.at[d], y_dev(d)).wait_recv()
    w_out[...] = w32[...] + at[...].astype(F32).T

    for copy in sends:
        copy.wait_send()


def finish(*refs):
    sources, results, sems = refs[:6], refs[6:12], refs[12]
    copies = [pltpu.make_async_copy(a, b, sems.at[i]) for i, (a, b) in enumerate(zip(sources, results))]
    for copy in copies:
        copy.start()
    for copy in copies:
        copy.wait()


def body(
    activations,
    cotangent,
    weight,
    first_moment,
    second_moment,
    anchor,
    outer_momentum,
    fragment_rows,
):
    hbm = pl.BlockSpec(memory_space=pltpu.HBM)
    held = pl.BlockSpec(memory_space=pltpu.VMEM)
    dma = pltpu.SemaphoreType.DMA
    vm = pltpu.VMEM
    shape = jax.ShapeDtypeStruct
    out_shape = (
        shape((ROWS, C), F32),
        shape((ROWS, C), F32),
        shape((ROWS, C), F32),
        shape((COLS, ROWS), F32),
        shape((COLS, ROWS), F32),
        shape((TOK, C), BF),
    )
    results = pl.pallas_call(
        exchange,
        out_shape=tuple(vm(a.shape, a.dtype) for a in out_shape),
        in_specs=[hbm] * 8,
        out_specs=[held] * 6,
        scratch_shapes=[
            vm((ROWS, C), F32),
            vm((ROWS, C), F32),
            vm((ROWS, C), F32),
            vm((COLS, ROWS), F32),
            vm((COLS, ROWS), F32),
            vm((1, ROWS), jnp.int32),
            vm((4, 4 * TOK, ROWS), BF),
            vm((4 * TOK, C), BF),
            vm((4, ROWS, C), BF),
            vm((4 * TOK, C), F32),
            vm((3, ROWS, C), BF),
            vm((ROWS, C), BF),
            vm((ROWS, C), BF),
            vm((ROWS, C), BF),
            vm((ROWS, C), F32),
            vm((TOK, C), BF),
            vm((TOK, C), BF),
            vm((TOK, C), BF),
            vm((TOK, C), BF),
            vm((TOK, C), BF),
            vm((TOK, C), BF),
            vm((C, ROWS), BF),
            vm((NY, BAND, ROWS), BF),
            vm((BAND, ROWS), F32),
            vm((BAND, ROWS), BF),
            vm((NH, COLS, ROWS), BF),
            vm((C, ROWS), BF),
            vm((ROWS, 128), F32),
            dma((11,)),
            dma((4 * UNITS, 3)),
            dma((4 * UNITS, 3)),
            dma((3,)),
            dma((3,)),
            dma((3,)),
            dma((3,)),
            dma((3,)),
            dma((3,)),
            dma((len(PARTS),)),
            dma((len(PARTS),)),
            dma((len(PARTS),)),
            dma((len(PARTS),)),
            dma((len(PARTS),)),
            dma((len(PARTS),)),
            dma((NY,)),
            dma((NY,)),
            dma((NH,)),
            dma((NH,)),
            dma((NH,)),
            dma((NH,)),
            dma((NY,)),
            dma((NY,)),
        ],
        compiler_params=pltpu.CompilerParams(
            collective_id=0, has_side_effects=True, vmem_limit_bytes=32 * 1024 * 1024
        ),
        name="exchange",
    )(
        *(
            pltpu.with_memory_space_constraint(a, pltpu.HBM)
            for a in (
                activations[0],
                cotangent[0],
                weight[0],
                anchor.T,
                outer_momentum.T,
                fragment_rows[None, :],
                first_moment[0],
                second_moment[0],
            )
        )
    )

    weight_out, first_new, second_new, anchor_new, momentum_new, projected = pl.pallas_call(
        finish,
        out_shape=out_shape,
        in_specs=[held] * 6,
        out_specs=[hbm] * 6,
        scratch_shapes=[dma((6,))],
        compiler_params=pltpu.CompilerParams(vmem_limit_bytes=8 * 1024 * 1024),
        name="finish",
    )(*(pltpu.with_memory_space_constraint(a, pltpu.VMEM) for a in results))
    return (
        weight_out[None],
        first_new[None],
        second_new[None],
        anchor_new.T,
        momentum_new.T,
        projected[None],
    )


def solution(mesh):
    return jax.shard_map(
        body,
        mesh=mesh,
        in_specs=(
            P("replica", "tensor", None),
            P("replica", "tensor", None),
            P("replica", "tensor", None),
            P("replica", "tensor", None),
            P("replica", "tensor", None),
            P("tensor", "replica"),
            P("tensor", "replica"),
            P("tensor"),
        ),
        out_specs=(
            P("replica", "tensor", None),
            P("replica", "tensor", None),
            P("replica", "tensor", None),
            P("tensor", "replica"),
            P("tensor", "replica"),
            P("replica", "tensor", None),
        ),
        check_vma=False,
    )
```

```python
import jax
import jax.numpy as jnp
from jax import lax
from jax.experimental import pallas as pl
from jax.experimental.pallas import tpu as pltpu
from jax.sharding import PartitionSpec as P

D = 4096
C = 512
STEP = 20
NX = 4
NY = 8
NH = 4
ROWS = 256
TOK = 192
COLS = 16
BAND = NH * COLS
SCALE = D ** (-0.5)

FIRST_DECAY = 0.9
SECOND_DECAY = 0.95
ADAM_EPS = 1e-08
INNER_RATE = 0.02
WEIGHT_DECAY = 0.1
OUTER_RATE = 0.7
OUTER_MU = 0.9
MIX_SHARE = 0.5

BF = jnp.bfloat16
F32 = jnp.float32
MESH = pl.DeviceIdType.MESH
AHEAD = 3
PLACES = (0, 2, 4)
PARTS = ((0, 96), (96, 96))


def exchange(
    act,
    cot,
    weight,
    anchor,
    mom,
    frag,
    first,
    second,
    w_out,
    first_out,
    second_out,
    anchor_out,
    mom_out,
    y_out,
    w32,
    f32,
    v32,
    old_anchor,
    old_mom,
    frag_v,
    xq,
    cq,
    wq,
    acc,
    g_send,
    g_opp,
    g_sum,
    g_dir,
    g_res,
    ym_out,
    ym_in,
    ys_out,
    ys_in,
    yf_out,
    yf_in,
    wt,
    ybuf,
    s32,
    s16,
    zbuf,
    at,
    m_res,
    act_v,
    local_sem,
    x_send,
    x_recv,
    c_send,
    c_recv,
    w_send,
    w_recv,
    gs_send,
    gs_recv,
    ym_send,
    ym_recv,
    ys_send,
    ys_recv,
    yf_send,
    yf_recv,
    r_send,
    r_recv,
    h_send,
    h_recv,
    b_send,
    b_recv,
    a_send,
    a_recv,
):
    rep = lax.axis_index("replica")
    ten = lax.axis_index("tensor")
    y, h = rep // NH, rep % NH
    x, z, c = ten // 4, (ten // 2) % 2, ten % 2
    pair = x // 2
    side = (x + pair) % 2
    place = pair + z * (3 - 2 * pair)
    q = side * 2 + c
    s = 1 - 2 * c

    def tensor_at(i, g, cc):
        zz = i // 2
        p = (i + zz) % 2
        return (g + p * (3 - 2 * g)) * 4 + zz * 2 + cc

    others = ((side, 1 - c), (1 - side, c), (1 - side, 1 - c))
    q_sib, q_far, q_diag = (g * 2 + cc for g, cc in others)
    sib, far, diag = ((rep, tensor_at(place, g, cc)) for g, cc in others)
    dev_ahead = (rep, tensor_at((place + s + NX) % NX, side, c))
    dev_behind = (rep, tensor_at((place - s + NX) % NX, side, c))

    def y_dev(d):
        return (((y + d) % NY) * NH + h, ten)

    def h_dev(d):
        return (y * NH + (h + d) % NH, ten)

    peers = [sib, far, diag, dev_ahead, dev_behind]
    peers += [y_dev(d) for d in range(1, NY)] + [h_dev(d) for d in range(1, NH)]
    y_order = (4, 3, 5, 2, 6, 1, 7)
    h_order = (2, 1, 3)
    barrier = pltpu.get_barrier_semaphore()
    for dev in peers:
        pl.semaphore_signal(barrier, inc=1, device_id=dev, device_id_type=MESH)

    def remote(src, dst, send, recv, dev):
        return pltpu.make_async_remote_copy(
            src_ref=src, dst_ref=dst, send_sem=send, recv_sem=recv, device_id=dev, device_id_type=MESH
        )

    def part(i, n):
        return pl.ds(pl.multiple_of(i * n, n), n)

    def tokens(qq, first_row, n):
        return pl.ds(pl.multiple_of(qq * TOK + first_row, 16), n)

    def x_cols(g, cc, j):
        ss = 1 - 2 * cc
        shift = (2, ss + NX, NX - ss, 0)[j]
        return part(tensor_at((place + shift) % NX, g, cc), ROWS)

    def local(src, dst, sem):
        copy = pltpu.make_async_copy(src, dst, sem)
        copy.start()
        return copy

    w_copy = local(weight, w32, local_sem.at[0])
    c_copy = local(cot, cq.at[part(q, TOK)], local_sem.at[1])
    x_copies = [local(act.at[:, x_cols(side, c, j)], xq.at[j, part(q, TOK)], local_sem.at[2 + j]) for j in range(4)]
    small_copies = [
        local(anchor, old_anchor, local_sem.at[6]),
        local(mom, old_mom, local_sem.at[7]),
        local(frag, frag_v, local_sem.at[8]),
    ]
    v_copy = local(act, act_v, local_sem.at[11])
    moment_copies = [local(first, f32, local_sem.at[9]), local(second, v32, local_sem.at[10])]

    pl.semaphore_wait(barrier, len(peers))

    sends = []

    def start(copy):
        copy.start()
        sends.append(copy)
        return copy

    targets = ((1, far, others[1]), (2, diag, others[2]), (0, sib, others[0]))

    def unit(u):
        return (u // 2, *PARTS[u % 2])

    def x_issue(u):
        j, r, n = unit(u)
        for e, dev, (g, cc) in targets:
            src = (act if u < AHEAD else act_v).at[pl.ds(r, n), x_cols(g, cc, j)]
            start(remote(src, xq.at[j, tokens(q, r, n)], x_send.at[u, e], x_recv.at[u, e], dev))

    def x_wait(u):
        j, r, n = unit(u)
        if r == 0:
            x_copies[j].wait()
        for e, qq in enumerate((q_sib, q_far, q_diag)):
            src = act.at[pl.ds(0, n), pl.ds(0, ROWS)]
            remote(src, xq.at[j, tokens(qq, r, n)], x_send.at[u, e], x_recv.at[u, e], sib).wait_recv()
        if u == 0:
            v_copy.wait()
        if u + AHEAD < 8:
            x_issue(u + AHEAD)

    def send_features():
        start(remote(cot, cq.at[part(q, TOK)], c_send.at[1], c_recv.at[1], far))
        start(remote(cot, cq.at[part(q, TOK)], c_send.at[0], c_recv.at[0], sib))
        for u in range(AHEAD):
            x_issue(u)

    stage_r = {}

    def send_columns():
        wt[...] = w32[...].T.astype(BF)
        for d in y_order:
            src = wt.at[part((y + d) % NY, BAND)]
            stage_r[d] = start(remote(src, ybuf.at[d], r_send.at[d], r_recv.at[d], y_dev(d)))

    send_features()
    w_copy.wait()
    wq[3] = w32[...].astype(BF)
    w_ahead = start(remote(wq.at[3], wq.at[2], w_send.at[0], w_recv.at[0], dev_ahead))
    w_behind = start(remote(wq.at[3], wq.at[1], w_send.at[1], w_recv.at[1], dev_behind))
    send_columns()
    for copy in small_copies:
        copy.wait()
    m_res[...] = jnp.broadcast_to((frag_v[...] == 1).astype(F32), (128, ROWS)).T

    w_ahead.wait_recv()
    w_pass = start(remote(wq.at[2], wq.at[0], w_send.at[2], w_recv.at[2], dev_ahead))
    remote(cot, cq.at[part(q_far, TOK)], c_send.at[1], c_recv.at[1], far).wait_recv()
    start(remote(cq.at[part(q_far, TOK)], cq.at[part(q_far, TOK)], c_send.at[2], c_recv.at[2], sib))

    def grad(j):
        return lax.dot_general(xq[j], cq[...], (((0,), (0,)), ((), ())), preferred_element_type=F32)

    def project(j):
        return jnp.dot(xq[j], wq[j], preferred_element_type=F32)

    stage_h = {}

    def sum_y():
        total = wt[part(y, BAND), :].astype(F32)
        for d in y_order:
            stage_r[d].wait_recv()
            total = total + ybuf[d].astype(F32)
        s32[...] = total
        s16[...] = total.astype(BF)
        for d in h_order:
            src = s16.at[part((h + d) % NH, COLS)]
            stage_h[d] = start(remote(src, zbuf.at[d], h_send.at[d], h_recv.at[d], h_dev(d)))

    def outer_step():
        total = s32[part(h, COLS), :]
        for d in h_order:
            stage_h[d].wait_recv()
            total = total + zbuf[d].astype(F32)
        inside = frag_v[...] == 1
        pseudo = old_anchor[...] - total * (1.0 / (NY * NH))
        momentum = OUTER_MU * old_mom[...] + pseudo
        moved = old_anchor[...] - OUTER_RATE * (pseudo + OUTER_MU * momentum)
        own = part(rep, COLS)
        at[own, :] = jnp.where(inside, MIX_SHARE * moved, 0.0).astype(BF)
        for d in h_order:
            start(remote(at.at[own], at.at[own], b_send.at[d], b_recv.at[d], h_dev(d)))
        anchor_out[...] = jnp.where(inside, moved, old_anchor[...])
        mom_out[...] = jnp.where(inside, momentum, old_mom[...])

    def gather_y():
        for d in h_order:
            theirs = part(y * NH + (h - d + NH) % NH, COLS)
            remote(at.at[theirs], at.at[theirs], b_send.at[d], b_recv.at[d], h_dev(d)).wait_recv()
        for d in y_order:
            start(remote(at.at[part(y, BAND)], at.at[part(y, BAND)], a_send.at[d], a_recv.at[d], y_dev(d)))

    def outer(u):
        for place, stage in zip(PLACES, (sum_y, outer_step, gather_y)):
            if place == u:
                stage()

    x_wait(0)
    outer(0)
    x_wait(1)
    remote(cot, cq.at[part(q_sib, TOK)], c_send.at[0], c_recv.at[0], sib).wait_recv()
    remote(cot, cq.at[part(q_diag, TOK)], c_send.at[2], c_recv.at[2], sib).wait_recv()
    c_copy.wait()
    g_send[0] = grad(0).astype(BF)
    to_opp = start(remote(g_send.at[0], g_opp, gs_send.at[0], gs_recv.at[0], dev_ahead))
    outer(1)

    x_wait(2)
    w_pass.wait_recv()
    acc[...] = project(0)
    outer(2)
    x_wait(3)
    g = grad(1)
    to_opp.wait_recv()
    g_send[1] = (g + g_opp[...].astype(F32)).astype(BF)
    to_ahead = start(remote(g_send.at[1], g_sum, gs_send.at[1], gs_recv.at[1], dev_ahead))
    outer(3)

    x_wait(4)
    w_behind.wait_recv()
    acc[...] += project(1)
    outer(4)
    x_wait(5)
    g_send[2] = grad(2).astype(BF)
    to_behind = start(remote(g_send.at[2], g_dir, gs_send.at[2], gs_recv.at[2], dev_behind))
    acc[...] += project(2)
    outer(5)

    def last(qq, r, n):
        rows = tokens(qq, r, n)
        return acc[rows, :] + jnp.dot(xq[3, rows, :], wq[3], preferred_element_type=F32)

    mids, sibs, fars = {}, {}, {}
    for k, (r, n) in enumerate(PARTS):
        here = pl.ds(r, n)
        x_wait(6 + k)
        ym_out[here, :] = last(q_diag, r, n).astype(BF)
        mids[k] = start(remote(ym_out.at[here], ym_in.at[here], ym_send.at[k], ym_recv.at[k], sib))
        ys_out[here, :] = last(q_sib, r, n).astype(BF)
        sibs[k] = start(remote(ys_out.at[here], ys_in.at[here], ys_send.at[k], ys_recv.at[k], sib))
        beyond = last(q_far, r, n)
        own_rows = tokens(q, r, n)
        acc[own_rows, :] = last(q, r, n)
        mids[k].wait_recv()
        yf_out[here, :] = (beyond + ym_in[here, :].astype(F32)).astype(BF)
        fars[k] = start(remote(yf_out.at[here], yf_in.at[here], yf_send.at[k], yf_recv.at[k], far))
        outer(6 + k)

    g_res[...] = grad(3)
    to_ahead.wait_recv()
    to_behind.wait_recv()
    for copy in moment_copies:
        copy.wait()

    def inner_step(i, carry):
        r = part(i, 32)
        gradient = (g_res[r, :] + g_sum[r, :].astype(F32) + g_dir[r, :].astype(F32)) * SCALE
        moment = FIRST_DECAY * f32[r, :] + (1.0 - FIRST_DECAY) * gradient
        square = SECOND_DECAY * v32[r, :] + (1.0 - SECOND_DECAY) * gradient * gradient
        first_out[r, :] = moment
        second_out[r, :] = square
        first_hat = moment / (1.0 - FIRST_DECAY**STEP)
        second_hat = square / (1.0 - SECOND_DECAY**STEP)
        update = first_hat / (jnp.sqrt(second_hat) + ADAM_EPS) + WEIGHT_DECAY * w32[r, :]
        inner = w32[r, :] - INNER_RATE * update
        share = 1.0 - MIX_SHARE * m_res[r, :][:, :1]
        w32[r, :] = inner * share
        return carry

    lax.fori_loop(0, ROWS // 32, inner_step, 0)

    for k, (r, n) in enumerate(PARTS):
        here = pl.ds(r, n)
        sibs[k].wait_recv()
        fars[k].wait_recv()
        total = acc[tokens(q, r, n), :] + ys_in[here, :].astype(F32) + yf_in[here, :].astype(F32)
        y_out[here, :] = (total * SCALE).astype(BF)

    for d in y_order:
        theirs = part((y - d + NY) % NY, BAND)
        remote(at.at[theirs], at.at[theirs], a_send.at[d], a_recv.at[d], y_dev(d)).wait_recv()
    w_out[...] = w32[...] + at[...].astype(F32).T

    for copy in sends:
        copy.wait_send()


def finish(*refs):
    sources, results, sems = refs[:6], refs[6:12], refs[12]
    copies = [pltpu.make_async_copy(a, b, sems.at[i]) for i, (a, b) in enumerate(zip(sources, results))]
    for copy in copies:
        copy.start()
    for copy in copies:
        copy.wait()


def body(
    activations,
    cotangent,
    weight,
    first_moment,
    second_moment,
    anchor,
    outer_momentum,
    fragment_rows,
):
    hbm = pl.BlockSpec(memory_space=pltpu.HBM)
    held = pl.BlockSpec(memory_space=pltpu.VMEM)
    dma = pltpu.SemaphoreType.DMA
    vm = pltpu.VMEM
    shape = jax.ShapeDtypeStruct
    out_shape = (
        shape((ROWS, C), F32),
        shape((ROWS, C), F32),
        shape((ROWS, C), F32),
        shape((COLS, ROWS), F32),
        shape((COLS, ROWS), F32),
        shape((TOK, C), BF),
    )
    results = pl.pallas_call(
        exchange,
        out_shape=tuple(vm(a.shape, a.dtype) for a in out_shape),
        in_specs=[hbm] * 8,
        out_specs=[held] * 6,
        scratch_shapes=[
            vm((ROWS, C), F32),
            vm((ROWS, C), F32),
            vm((ROWS, C), F32),
            vm((COLS, ROWS), F32),
            vm((COLS, ROWS), F32),
            vm((1, ROWS), jnp.int32),
            vm((4, 4 * TOK, ROWS), BF),
            vm((4 * TOK, C), BF),
            vm((4, ROWS, C), BF),
            vm((4 * TOK, C), F32),
            vm((3, ROWS, C), BF),
            vm((ROWS, C), BF),
            vm((ROWS, C), BF),
            vm((ROWS, C), BF),
            vm((ROWS, C), F32),
            vm((TOK, C), BF),
            vm((TOK, C), BF),
            vm((TOK, C), BF),
            vm((TOK, C), BF),
            vm((TOK, C), BF),
            vm((TOK, C), BF),
            vm((C, ROWS), BF),
            vm((NY, BAND, ROWS), BF),
            vm((BAND, ROWS), F32),
            vm((BAND, ROWS), BF),
            vm((NH, COLS, ROWS), BF),
            vm((C, ROWS), BF),
            vm((ROWS, 128), F32),
            vm((TOK, D), BF),
            dma((12,)),
            dma((8, 3)),
            dma((8, 3)),
            dma((3,)),
            dma((3,)),
            dma((3,)),
            dma((3,)),
            dma((3,)),
            dma((3,)),
            dma((len(PARTS),)),
            dma((len(PARTS),)),
            dma((len(PARTS),)),
            dma((len(PARTS),)),
            dma((len(PARTS),)),
            dma((len(PARTS),)),
            dma((NY,)),
            dma((NY,)),
            dma((NH,)),
            dma((NH,)),
            dma((NH,)),
            dma((NH,)),
            dma((NY,)),
            dma((NY,)),
        ],
        compiler_params=pltpu.CompilerParams(
            collective_id=0, has_side_effects=True, vmem_limit_bytes=32 * 1024 * 1024
        ),
        name="exchange",
    )(
        *(
            pltpu.with_memory_space_constraint(a, pltpu.HBM)
            for a in (
                activations[0],
                cotangent[0],
                weight[0],
                anchor.T,
                outer_momentum.T,
                fragment_rows[None, :],
                first_moment[0],
                second_moment[0],
            )
        )
    )

    weight_out, first_new, second_new, anchor_new, momentum_new, projected = pl.pallas_call(
        finish,
        out_shape=out_shape,
        in_specs=[held] * 6,
        out_specs=[hbm] * 6,
        scratch_shapes=[dma((6,))],
        compiler_params=pltpu.CompilerParams(vmem_limit_bytes=8 * 1024 * 1024),
        name="finish",
    )(*(pltpu.with_memory_space_constraint(a, pltpu.VMEM) for a in results))
    return (
        weight_out[None],
        first_new[None],
        second_new[None],
        anchor_new.T,
        momentum_new.T,
        projected[None],
    )


def solution(mesh):
    return jax.shard_map(
        body,
        mesh=mesh,
        in_specs=(
            P("replica", "tensor", None),
            P("replica", "tensor", None),
            P("replica", "tensor", None),
            P("replica", "tensor", None),
            P("replica", "tensor", None),
            P("tensor", "replica"),
            P("tensor", "replica"),
            P("tensor"),
        ),
        out_specs=(
            P("replica", "tensor", None),
            P("replica", "tensor", None),
            P("replica", "tensor", None),
            P("tensor", "replica"),
            P("tensor", "replica"),
            P("replica", "tensor", None),
        ),
        check_vma=False,
    )
```

```python
import jax
import jax.numpy as jnp
from jax import lax
from jax.experimental import pallas as pl
from jax.experimental.pallas import tpu as pltpu
from jax.sharding import PartitionSpec as P

D = 4096
C = 512
STEP = 20
NX = 4
NY = 8
NH = 4
ROWS = 256
TOK = 192
COLS = 16
BAND = NH * COLS
SCALE = D ** (-0.5)

FIRST_DECAY = 0.9
SECOND_DECAY = 0.95
ADAM_EPS = 1e-08
INNER_RATE = 0.02
WEIGHT_DECAY = 0.1
OUTER_RATE = 0.7
OUTER_MU = 0.9
MIX_SHARE = 0.5

BF = jnp.bfloat16
F32 = jnp.float32
MESH = pl.DeviceIdType.MESH
AHEAD = 3
PLACES = (0, 2, 4)
PARTS = ((0, 96), (96, 96))


def exchange(
    act,
    cot,
    weight,
    anchor,
    mom,
    frag,
    first,
    second,
    w_out,
    first_out,
    second_out,
    anchor_out,
    mom_out,
    y_out,
    w32,
    f32,
    v32,
    old_anchor,
    old_mom,
    frag_v,
    xq,
    cq,
    wq,
    acc,
    g_send,
    g_opp,
    g_sum,
    g_dir,
    g_res,
    ym_out,
    ym_in,
    ys_out,
    ys_in,
    yf_out,
    yf_in,
    wt,
    ybuf,
    s32,
    s16,
    zbuf,
    at,
    m_res,
    act_v,
    local_sem,
    x_send,
    x_recv,
    c_send,
    c_recv,
    w_send,
    w_recv,
    gs_send,
    gs_recv,
    ym_send,
    ym_recv,
    ys_send,
    ys_recv,
    yf_send,
    yf_recv,
    r_send,
    r_recv,
    h_send,
    h_recv,
    b_send,
    b_recv,
    a_send,
    a_recv,
):
    rep = lax.axis_index("replica")
    ten = lax.axis_index("tensor")
    y, h = rep // NH, rep % NH
    x, z, c = ten // 4, (ten // 2) % 2, ten % 2
    pair = x // 2
    side = (x + pair) % 2
    place = pair + z * (3 - 2 * pair)
    q = side * 2 + c
    s = 1 - 2 * c

    def tensor_at(i, g, cc):
        zz = i // 2
        p = (i + zz) % 2
        return (g + p * (3 - 2 * g)) * 4 + zz * 2 + cc

    others = ((side, 1 - c), (1 - side, c), (1 - side, 1 - c))
    q_sib, q_far, q_diag = (g * 2 + cc for g, cc in others)
    sib, far, diag = ((rep, tensor_at(place, g, cc)) for g, cc in others)
    dev_ahead = (rep, tensor_at((place + s + NX) % NX, side, c))
    dev_behind = (rep, tensor_at((place - s + NX) % NX, side, c))

    def y_dev(d):
        return (((y + d) % NY) * NH + h, ten)

    def h_dev(d):
        return (y * NH + (h + d) % NH, ten)

    peers = [sib, far, diag, dev_ahead, dev_behind]
    peers += [y_dev(d) for d in range(1, NY)] + [h_dev(d) for d in range(1, NH)]
    y_order = (4, 3, 5, 2, 6, 1, 7)
    h_order = (2, 1, 3)
    barrier = pltpu.get_barrier_semaphore()
    for dev in peers:
        pl.semaphore_signal(barrier, inc=1, device_id=dev, device_id_type=MESH)

    def remote(src, dst, send, recv, dev):
        return pltpu.make_async_remote_copy(
            src_ref=src, dst_ref=dst, send_sem=send, recv_sem=recv, device_id=dev, device_id_type=MESH
        )

    def part(i, n):
        return pl.ds(pl.multiple_of(i * n, n), n)

    def tokens(qq, first_row, n):
        return pl.ds(pl.multiple_of(qq * TOK + first_row, 16), n)

    def x_cols(g, cc, j):
        ss = 1 - 2 * cc
        shift = (2, ss + NX, NX - ss, 0)[j]
        return part(tensor_at((place + shift) % NX, g, cc), ROWS)

    def local(src, dst, sem):
        copy = pltpu.make_async_copy(src, dst, sem)
        copy.start()
        return copy

    w_copy = local(weight, w32, local_sem.at[0])
    c_copy = local(cot, cq.at[part(q, TOK)], local_sem.at[1])
    x_copies = [local(act.at[:, x_cols(side, c, j)], xq.at[j, part(q, TOK)], local_sem.at[2 + j]) for j in range(4)]
    small_copies = [
        local(anchor, old_anchor, local_sem.at[6]),
        local(mom, old_mom, local_sem.at[7]),
        local(frag, frag_v, local_sem.at[8]),
    ]
    v_copy = local(act, act_v, local_sem.at[11])
    moment_copies = [local(first, f32, local_sem.at[9]), local(second, v32, local_sem.at[10])]

    pl.semaphore_wait(barrier, len(peers))

    sends = []

    def start(copy):
        copy.start()
        sends.append(copy)
        return copy

    targets = ((1, far, others[1]), (2, diag, others[2]), (0, sib, others[0]))

    def unit(u):
        return (u // 2, *PARTS[u % 2])

    def x_issue(u):
        j, r, n = unit(u)
        for e, dev, (g, cc) in targets:
            src = (act if u < AHEAD else act_v).at[pl.ds(r, n), x_cols(g, cc, j)]
            start(remote(src, xq.at[j, tokens(q, r, n)], x_send.at[u, e], x_recv.at[u, e], dev))

    def x_wait(u):
        j, r, n = unit(u)
        if r == 0:
            x_copies[j].wait()
        for e, qq in enumerate((q_sib, q_far, q_diag)):
            src = act.at[pl.ds(0, n), pl.ds(0, ROWS)]
            remote(src, xq.at[j, tokens(qq, r, n)], x_send.at[u, e], x_recv.at[u, e], sib).wait_recv()
        if u == 0:
            v_copy.wait()
        if u + AHEAD < 8:
            x_issue(u + AHEAD)

    def send_features():
        start(remote(cot, cq.at[part(q, TOK)], c_send.at[1], c_recv.at[1], far))
        start(remote(cot, cq.at[part(q, TOK)], c_send.at[0], c_recv.at[0], sib))
        for u in range(AHEAD):
            x_issue(u)

    stage_r = {}

    def send_columns():
        wt[...] = w32[...].T.astype(BF)
        for d in y_order:
            src = wt.at[part((y + d) % NY, BAND)]
            stage_r[d] = start(remote(src, ybuf.at[d], r_send.at[d], r_recv.at[d], y_dev(d)))

    send_features()
    w_copy.wait()
    wq[3] = w32[...].astype(BF)
    w_ahead = start(remote(wq.at[3], wq.at[2], w_send.at[0], w_recv.at[0], dev_ahead))
    w_behind = start(remote(wq.at[3], wq.at[1], w_send.at[1], w_recv.at[1], dev_behind))
    send_columns()
    for copy in small_copies:
        copy.wait()
    m_res[...] = jnp.broadcast_to((frag_v[...] == 1).astype(F32), (128, ROWS)).T

    w_ahead.wait_recv()
    w_pass = start(remote(wq.at[2], wq.at[0], w_send.at[2], w_recv.at[2], dev_ahead))
    remote(cot, cq.at[part(q_far, TOK)], c_send.at[1], c_recv.at[1], far).wait_recv()
    start(remote(cq.at[part(q_far, TOK)], cq.at[part(q_far, TOK)], c_send.at[2], c_recv.at[2], sib))

    def grad(j):
        return lax.dot_general(xq[j], cq[...], (((0,), (0,)), ((), ())), preferred_element_type=F32)

    def project(j):
        return jnp.dot(xq[j], wq[j], preferred_element_type=F32)

    stage_h = {}

    def sum_y():
        total = wt[part(y, BAND), :].astype(F32)
        for d in y_order:
            stage_r[d].wait_recv()
            total = total + ybuf[d].astype(F32)
        s32[...] = total
        s16[...] = total.astype(BF)
        for d in h_order:
            src = s16.at[part((h + d) % NH, COLS)]
            stage_h[d] = start(remote(src, zbuf.at[d], h_send.at[d], h_recv.at[d], h_dev(d)))

    def outer_step():
        total = s32[part(h, COLS), :]
        for d in h_order:
            stage_h[d].wait_recv()
            total = total + zbuf[d].astype(F32)
        inside = frag_v[...] == 1
        pseudo = old_anchor[...] - total * (1.0 / (NY * NH))
        momentum = OUTER_MU * old_mom[...] + pseudo
        moved = old_anchor[...] - OUTER_RATE * (pseudo + OUTER_MU * momentum)
        own = part(rep, COLS)
        at[own, :] = jnp.where(inside, MIX_SHARE * moved, 0.0).astype(BF)
        for d in h_order:
            start(remote(at.at[own], at.at[own], b_send.at[d], b_recv.at[d], h_dev(d)))
        anchor_out[...] = jnp.where(inside, moved, old_anchor[...])
        mom_out[...] = jnp.where(inside, momentum, old_mom[...])

    def gather_y():
        for d in h_order:
            theirs = part(y * NH + (h - d + NH) % NH, COLS)
            remote(at.at[theirs], at.at[theirs], b_send.at[d], b_recv.at[d], h_dev(d)).wait_recv()
        for d in y_order:
            start(remote(at.at[part(y, BAND)], at.at[part(y, BAND)], a_send.at[d], a_recv.at[d], y_dev(d)))

    def outer(u):
        for place, stage in zip(PLACES, (sum_y, outer_step, gather_y)):
            if place == u:
                stage()

    x_wait(0)
    outer(0)
    x_wait(1)
    remote(cot, cq.at[part(q_sib, TOK)], c_send.at[0], c_recv.at[0], sib).wait_recv()
    remote(cot, cq.at[part(q_diag, TOK)], c_send.at[2], c_recv.at[2], sib).wait_recv()
    c_copy.wait()
    g_send[0] = grad(0).astype(BF)
    to_opp = start(remote(g_send.at[0], g_opp, gs_send.at[0], gs_recv.at[0], dev_ahead))
    outer(1)

    x_wait(2)
    w_pass.wait_recv()
    acc[...] = project(0)
    outer(2)
    x_wait(3)
    g = grad(1)
    to_opp.wait_recv()
    g_send[1] = (g + g_opp[...].astype(F32)).astype(BF)
    to_ahead = start(remote(g_send.at[1], g_sum, gs_send.at[1], gs_recv.at[1], dev_ahead))
    outer(3)

    x_wait(4)
    w_behind.wait_recv()
    acc[...] += project(1)
    outer(4)
    x_wait(5)
    g_send[2] = grad(2).astype(BF)
    to_behind = start(remote(g_send.at[2], g_dir, gs_send.at[2], gs_recv.at[2], dev_behind))
    acc[...] += project(2)
    outer(5)

    def last(qq, r, n):
        rows = tokens(qq, r, n)
        return acc[rows, :] + jnp.dot(xq[3, rows, :], wq[3], preferred_element_type=F32)

    mids, sibs, fars = {}, {}, {}
    for k, (r, n) in enumerate(PARTS):
        here = pl.ds(r, n)
        x_wait(6 + k)
        ym_out[here, :] = last(q_diag, r, n).astype(BF)
        mids[k] = start(remote(ym_out.at[here], ym_in.at[here], ym_send.at[k], ym_recv.at[k], sib))
        ys_out[here, :] = last(q_sib, r, n).astype(BF)
        sibs[k] = start(remote(ys_out.at[here], ys_in.at[here], ys_send.at[k], ys_recv.at[k], sib))
        beyond = last(q_far, r, n)
        own_rows = tokens(q, r, n)
        acc[own_rows, :] = last(q, r, n)
        mids[k].wait_recv()
        yf_out[here, :] = (beyond + ym_in[here, :].astype(F32)).astype(BF)
        fars[k] = start(remote(yf_out.at[here], yf_in.at[here], yf_send.at[k], yf_recv.at[k], far))
        outer(6 + k)

    g_res[...] = grad(3)
    to_ahead.wait_recv()
    to_behind.wait_recv()
    for copy in moment_copies:
        copy.wait()

    def inner_step(i, carry):
        r = part(i, 32)
        gradient = (g_res[r, :] + g_sum[r, :].astype(F32) + g_dir[r, :].astype(F32)) * SCALE
        moment = FIRST_DECAY * f32[r, :] + (1.0 - FIRST_DECAY) * gradient
        square = SECOND_DECAY * v32[r, :] + (1.0 - SECOND_DECAY) * gradient * gradient
        first_out[r, :] = moment
        second_out[r, :] = square
        first_hat = moment / (1.0 - FIRST_DECAY**STEP)
        second_hat = square / (1.0 - SECOND_DECAY**STEP)
        update = first_hat / (jnp.sqrt(second_hat) + ADAM_EPS) + WEIGHT_DECAY * w32[r, :]
        inner = w32[r, :] - INNER_RATE * update
        share = 1.0 - MIX_SHARE * m_res[r, :][:, :1]
        w32[r, :] = inner * share
        return carry

    lax.fori_loop(0, ROWS // 32, inner_step, 0)

    last_sums = sends.pop()
    for copy in sends:
        copy.wait_send()

    for k, (r, n) in enumerate(PARTS):
        here = pl.ds(r, n)
        sibs[k].wait_recv()
        fars[k].wait_recv()
        total = acc[tokens(q, r, n), :] + ys_in[here, :].astype(F32) + yf_in[here, :].astype(F32)
        y_out[here, :] = (total * SCALE).astype(BF)

    for d in y_order:
        theirs = part((y - d + NY) % NY, BAND)
        remote(at.at[theirs], at.at[theirs], a_send.at[d], a_recv.at[d], y_dev(d)).wait_recv()
    w_out[...] = w32[...] + at[...].astype(F32).T

    last_sums.wait_send()


def finish(*refs):
    sources, results, sems = refs[:6], refs[6:12], refs[12]
    copies = [pltpu.make_async_copy(a, b, sems.at[i]) for i, (a, b) in enumerate(zip(sources, results))]
    for copy in copies:
        copy.start()
    for copy in copies:
        copy.wait()


def body(
    activations,
    cotangent,
    weight,
    first_moment,
    second_moment,
    anchor,
    outer_momentum,
    fragment_rows,
):
    hbm = pl.BlockSpec(memory_space=pltpu.HBM)
    held = pl.BlockSpec(memory_space=pltpu.VMEM)
    dma = pltpu.SemaphoreType.DMA
    vm = pltpu.VMEM
    shape = jax.ShapeDtypeStruct
    out_shape = (
        shape((ROWS, C), F32),
        shape((ROWS, C), F32),
        shape((ROWS, C), F32),
        shape((COLS, ROWS), F32),
        shape((COLS, ROWS), F32),
        shape((TOK, C), BF),
    )
    results = pl.pallas_call(
        exchange,
        out_shape=tuple(vm(a.shape, a.dtype) for a in out_shape),
        in_specs=[hbm] * 8,
        out_specs=[held] * 6,
        scratch_shapes=[
            vm((ROWS, C), F32),
            vm((ROWS, C), F32),
            vm((ROWS, C), F32),
            vm((COLS, ROWS), F32),
            vm((COLS, ROWS), F32),
            vm((1, ROWS), jnp.int32),
            vm((4, 4 * TOK, ROWS), BF),
            vm((4 * TOK, C), BF),
            vm((4, ROWS, C), BF),
            vm((4 * TOK, C), F32),
            vm((3, ROWS, C), BF),
            vm((ROWS, C), BF),
            vm((ROWS, C), BF),
            vm((ROWS, C), BF),
            vm((ROWS, C), F32),
            vm((TOK, C), BF),
            vm((TOK, C), BF),
            vm((TOK, C), BF),
            vm((TOK, C), BF),
            vm((TOK, C), BF),
            vm((TOK, C), BF),
            vm((C, ROWS), BF),
            vm((NY, BAND, ROWS), BF),
            vm((BAND, ROWS), F32),
            vm((BAND, ROWS), BF),
            vm((NH, COLS, ROWS), BF),
            vm((C, ROWS), BF),
            vm((ROWS, 128), F32),
            vm((TOK, D), BF),
            dma((12,)),
            dma((8, 3)),
            dma((8, 3)),
            dma((3,)),
            dma((3,)),
            dma((3,)),
            dma((3,)),
            dma((3,)),
            dma((3,)),
            dma((len(PARTS),)),
            dma((len(PARTS),)),
            dma((len(PARTS),)),
            dma((len(PARTS),)),
            dma((len(PARTS),)),
            dma((len(PARTS),)),
            dma((NY,)),
            dma((NY,)),
            dma((NH,)),
            dma((NH,)),
            dma((NH,)),
            dma((NH,)),
            dma((NY,)),
            dma((NY,)),
        ],
        compiler_params=pltpu.CompilerParams(
            collective_id=0, has_side_effects=True, vmem_limit_bytes=32 * 1024 * 1024
        ),
        name="exchange",
    )(
        *(
            pltpu.with_memory_space_constraint(a, pltpu.HBM)
            for a in (
                activations[0],
                cotangent[0],
                weight[0],
                anchor.T,
                outer_momentum.T,
                fragment_rows[None, :],
                first_moment[0],
                second_moment[0],
            )
        )
    )

    weight_out, first_new, second_new, anchor_new, momentum_new, projected = pl.pallas_call(
        finish,
        out_shape=out_shape,
        in_specs=[held] * 6,
        out_specs=[hbm] * 6,
        scratch_shapes=[dma((6,))],
        compiler_params=pltpu.CompilerParams(vmem_limit_bytes=8 * 1024 * 1024),
        name="finish",
    )(*(pltpu.with_memory_space_constraint(a, pltpu.VMEM) for a in results))
    return (
        weight_out[None],
        first_new[None],
        second_new[None],
        anchor_new.T,
        momentum_new.T,
        projected[None],
    )


def solution(mesh):
    return jax.shard_map(
        body,
        mesh=mesh,
        in_specs=(
            P("replica", "tensor", None),
            P("replica", "tensor", None),
            P("replica", "tensor", None),
            P("replica", "tensor", None),
            P("replica", "tensor", None),
            P("tensor", "replica"),
            P("tensor", "replica"),
            P("tensor"),
        ),
        out_specs=(
            P("replica", "tensor", None),
            P("replica", "tensor", None),
            P("replica", "tensor", None),
            P("tensor", "replica"),
            P("tensor", "replica"),
            P("replica", "tensor", None),
        ),
        check_vma=False,
    )
```
